32 devices in a mesh: groups: 2 (over y), leaf: 4 (over z), sub: 2 (over x), col: 2 (over core).
Axes of the slice: x: 2, y: 2, z: 4, core: 2. Of those that a mesh axis runs over, the one named last changes fastest.
Arguments:
- incident: bfloat16 [2, 4096, 2048], P(None, ('leaf', 'sub'), ('groups', 'col')), parts along dimension 2, may hold values from -6 to 6
- self_weight: bfloat16 [10, 2, 32, 128, 128], P('groups', None, ('leaf', 'sub')), parts along dimension 0, may hold values from -0.3125 to 0.3125
- cross_weight: bfloat16 [10, 2, 32, 64, 128], P('groups', None, ('leaf', 'sub')), parts along dimension 0, may hold values from -0.4375 to 0.4375
- coupling: int32 [10, 32], P('groups', ('leaf', 'sub')), parts along dimension 0, may hold values 0 or 1
- block_ranks: int32 [10, 32], P('groups', ('leaf', 'sub')), parts along dimension 0, may hold values from 16 to 64
- leaf_order: int32 [64, 128], P(('groups', 'leaf', 'sub')), parts along dimension 0, may hold values from 0 to 127, each once within a row
Outputs:
- scattered: bfloat16 [2, 4096, 2048], P(None, ('leaf', 'sub'), ('groups', 'col')), parts along dimension 2
The draws below stay inside these ranges and needn't reach their ends.
There are 2 independent parts, one for each index of `groups`. The reference program is written for one: setup_inputs(seed, part) draws one part's arguments, and reference() takes and returns one part's arrays. A program takes and returns all parts, laid end to end along the dimension named above; each array names one. Nothing has to cross between parts.
All inputs are finite; a program needn't handle non-finite values. No bound on the sum of `coupling` on one device may be relied on, other than what follows from the above.
Results may differ from the reference program's by a relative error of at most 0.007.
Values may be sent and summed in bfloat16 or wider, within the bound.
A program may use at most 64 MiB of HBM per device.

```python
import jax
import jax.numpy as jnp

R = 128
RMAX = 64
LEVELS = 5
NBLK = 32
UNKNOWNS = 4096
COLS = 1024


def plant(entries, own_key, smallest, top_value):
    place = [jax.random.randint(jax.random.fold_in(own_key, axis), (), 0, length) for axis, length in enumerate(entries.shape)]
    longest = entries.shape.index(max(entries.shape))
    beside = place[:longest] + [(place[longest] + 1) % entries.shape[longest]] + place[longest + 1:]
    return entries.at[tuple(place)].set(smallest).at[tuple(beside)].set(top_value)


def levels(stream_key, dims, cuts, smallest, high):
    level = 1.0
    for axis_at, blocks in cuts:
        draws = jax.random.uniform(jax.random.fold_in(jax.random.fold_in(stream_key, 6), axis_at), (blocks,), jnp.float32, smallest / len(cuts), high / len(cuts))
        level = level * jnp.repeat(jnp.exp(draws), dims[axis_at] // blocks).reshape((-1,) + (1,) * (len(dims) - 1 - axis_at))
    return level


def gaussian(own_key, dims, scale, most, split=(), kind=jnp.bfloat16):
    drawn = scale * jax.random.normal(own_key, dims, jnp.float32)
    if split:
        drawn = drawn * levels(own_key, dims, split, -0.22, 0.18)
    return jnp.clip(drawn, -most, most).astype(kind)


def setup_inputs(seed: int = 0, part: int = 0) -> dict:
    streams_of = jax.random.split(jax.random.key(seed), 7)
    own_keys = jax.random.split(jax.random.fold_in(streams_of[6], part), 7)
    incident = gaussian(own_keys[0], (2, UNKNOWNS, COLS), 1.0, 6.0, ((1, 8), (2, 2)))
    self_weight = gaussian(own_keys[1], (LEVELS, 2, NBLK, R, R), (3 * R) ** -0.5, 0.3125, ((2, 8),))
    cross_weight = gaussian(own_keys[2], (LEVELS, 2, NBLK, RMAX, R), (3 * RMAX) ** -0.5, 0.4375, ((2, 8),))
    coupling = plant((jax.random.randint(own_keys[3], (LEVELS, NBLK), 0, 4) < 3).astype(jnp.int32), jax.random.fold_in(own_keys[3], 1), 0, 1)
    block_ranks = plant(jax.random.randint(own_keys[4], (LEVELS, NBLK), RMAX // 4, RMAX + 1), jax.random.fold_in(own_keys[4], 1), RMAX // 4, RMAX).astype(jnp.int32)
    leaf_order = jax.vmap(lambda own: jax.random.permutation(own, R))(jax.random.split(own_keys[5], NBLK)).reshape((NBLK, R)).astype(jnp.int32)
    return dict(incident=incident, self_weight=self_weight, cross_weight=cross_weight, coupling=coupling, block_ranks=block_ranks, leaf_order=leaf_order)


def complex_product(weight, field, form):
    weight_f = weight.astype(jnp.float32)
    field_f = field.astype(jnp.float32)
    real_part = jnp.einsum(form, weight_f[0], field_f[0]) - jnp.einsum(form, weight_f[1], field_f[1])
    imag_part = jnp.einsum(form, weight_f[0], field_f[1]) + jnp.einsum(form, weight_f[1], field_f[0])
    return jnp.stack([real_part, imag_part])


def reference(incident, self_weight, cross_weight, coupling, block_ranks, leaf_order):
    field = incident.reshape(2, NBLK, R, COLS)
    order_index = jnp.broadcast_to(leaf_order[None, :, :, None], field.shape)
    field = jnp.take_along_axis(field, order_index, axis=2)
    rank_index = jnp.arange(RMAX, dtype=jnp.int32)
    for level_index in range(LEVELS):
        stride = 2 ** level_index
        sibling = field.reshape(2, NBLK // (2 * stride), 2, stride, R, COLS)[:, :, ::-1]
        sibling = sibling.reshape(2, NBLK, R, COLS)[:, :, :RMAX]
        coupled = (rank_index[None, :] < block_ranks[level_index][:, None]) & (coupling[level_index][:, None] == 1)
        masked = cross_weight[level_index] * coupled[None, :, :, None].astype(jnp.bfloat16)
        own_term = complex_product(self_weight[level_index], field, "bij,bjn->bin")
        cross_term = complex_product(masked, sibling, "bki,bkn->bin")
        field = (own_term + cross_term).astype(jnp.bfloat16)
    return field.reshape(2, UNKNOWNS, COLS)
```

```python
import jax
import jax.numpy as jnp
from jax import lax
from jax.sharding import PartitionSpec as P


def from_partner(x, axis, stride):
    return lax.ppermute(x, axis, [(i, i ^ 1 << stride) for i in range(lax.axis_size(axis))])


def level_matrix(self_weight, cross_weight, coupling, block_ranks, level_index):
    lead_rows = cross_weight.shape[3]
    rank_index = jnp.arange(lead_rows, dtype=jnp.int32)
    coupled = (rank_index[None, :] < block_ranks[level_index][:, None]) & (
        coupling[level_index][:, None] == 1
    )
    masked = cross_weight[level_index] * coupled[None, :, :, None].astype(jnp.bfloat16)
    cross_t = jnp.swapaxes(masked, 2, 3)
    own = self_weight[level_index]
    upper = jnp.concatenate([own[0], -own[1], cross_t[0], -cross_t[1]], axis=2)
    lower = jnp.concatenate([own[1], own[0], cross_t[1], cross_t[0]], axis=2)
    return jnp.concatenate([upper, lower], axis=1)


def apply_level(field, sibling, self_weight, cross_weight, coupling, block_ranks, level_index):
    blocks = field.shape[0]
    block_rows = field.shape[2]
    columns = field.shape[3]
    lead_rows = sibling.shape[2]
    matrix = level_matrix(self_weight, cross_weight, coupling, block_ranks, level_index)
    stacked = jnp.concatenate(
        [
            field.reshape(blocks, 2 * block_rows, columns),
            sibling.reshape(blocks, 2 * lead_rows, columns),
        ],
        axis=1,
    )
    result = jnp.einsum("bij,bjn->bin", matrix, stacked, preferred_element_type=jnp.float32)
    return result.astype(jnp.bfloat16).reshape(blocks, 2, block_rows, columns)


def shards(incident, self_weight, cross_weight, coupling, block_ranks, leaf_order):
    blocks = leaf_order.shape[0]
    block_rows = leaf_order.shape[1]
    columns = incident.shape[2]
    lead_rows = cross_weight.shape[3]
    row_index = jnp.arange(block_rows, dtype=jnp.int32)
    selector = (leaf_order[:, :, None] == row_index[None, None, :]).astype(jnp.bfloat16)
    field = incident.reshape(2, blocks, block_rows, columns)
    field = jnp.einsum(
        "irk,cikn->icrn", selector, field, preferred_element_type=jnp.float32
    ).astype(jnp.bfloat16)
    local_bits = blocks.bit_length() - 1
    sub_bits = lax.axis_size("sub").bit_length() - 1
    leaf_bits = lax.axis_size("leaf").bit_length() - 1
    level_index = 0
    for which_bit in range(local_bits):
        stride = 2**which_bit
        sibling = field.reshape(blocks // (2 * stride), 2, stride, 2, block_rows, columns)[:, ::-1]
        sibling = sibling.reshape(blocks, 2, block_rows, columns)[:, :, :lead_rows]
        field = apply_level(
            field, sibling, self_weight, cross_weight, coupling, block_ranks, level_index
        )
        level_index += 1
    for which_bit in range(sub_bits):
        sibling = from_partner(field[:, :, :lead_rows], "sub", which_bit)
        field = apply_level(
            field, sibling, self_weight, cross_weight, coupling, block_ranks, level_index
        )
        level_index += 1
    for which_bit in range(leaf_bits):
        sibling = from_partner(field[:, :, :lead_rows], "leaf", which_bit)
        field = apply_level(
            field, sibling, self_weight, cross_weight, coupling, block_ranks, level_index
        )
        level_index += 1
    field = jnp.transpose(field, (1, 0, 2, 3))
    return field.reshape(2, blocks * block_rows, columns)


def solution(mesh):
    in_specs = (
        P(None, ("leaf", "sub"), ("groups", "col")),
        P("groups", None, ("leaf", "sub"), None, None),
        P("groups", None, ("leaf", "sub"), None, None),
        P("groups", ("leaf", "sub")),
        P("groups", ("leaf", "sub")),
        P(("groups", "leaf", "sub"), None),
    )
    out_specs = P(None, ("leaf", "sub"), ("groups", "col"))
    return jax.shard_map(shards, mesh=mesh, in_specs=in_specs, out_specs=out_specs, check_vma=False)
```

```python
import functools

import jax
import jax.numpy as jnp
from jax import lax
from jax.experimental import pallas as pl
from jax.experimental.pallas import tpu as pltpu
from jax.sharding import PartitionSpec as P

MESH = pl.DeviceIdType.MESH
WIDTH = 256
LAG = 2


def remote_levels():
    steps = []
    for axis in ("sub", "leaf"):
        for which_bit in range(lax.axis_size(axis).bit_length() - 1):
            steps.append((axis, 2**which_bit))
    return steps


def partner_of(axis, stride):
    me = lax.axis_index(axis)
    return {axis: me + stride * (1 - 2 * ((me // stride) % 2))}


def kernel(
    remote,
    ranks_ref,
    coupling_ref,
    order_ref,
    incident_ref,
    self_ref,
    cross_ref,
    out_ref,
    panel,
    weight,
    cross,
    own_matrix,
    cross_matrix,
    field,
    arrived,
    result,
    panel_sem,
    weight_sem,
    cross_sem,
    send_sem,
    recv_sem,
    out_sem,
):
    n_levels, _, blocks, rows, _ = weight.shape
    lead = cross.shape[3]
    chunks = panel.shape[0]
    width = panel.shape[4]
    local = n_levels - len(remote)
    partners = [partner_of(axis, stride) for axis, stride in remote]

    barrier = pltpu.get_barrier_semaphore()
    for partner in partners:
        pl.semaphore_signal(barrier, inc=1, device_id=partner, device_id_type=MESH)

    def load_panel(chunk):
        columns = pl.ds(chunk * width, width)
        return [
            pltpu.make_async_copy(
                incident_ref.at[:, pl.ds(block * rows, rows), columns],
                panel.at[chunk, block],
                panel_sem.at[chunk, block],
            )
            for block in range(blocks)
        ]

    def load_weight(level):
        return [
            pltpu.make_async_copy(self_ref.at[level], weight.at[level], weight_sem.at[level]),
            pltpu.make_async_copy(cross_ref.at[level], cross.at[level], cross_sem.at[level]),
        ]

    panels = [load_panel(chunk) for chunk in range(chunks)]
    weights = [load_weight(level) for level in range(n_levels)]
    for copy in panels[0]:
        copy.start()
    for level in range(local):
        for copy in weights[level]:
            copy.start()
    for chunk in range(1, chunks):
        for copy in panels[chunk]:
            copy.start()
    for level in range(local, n_levels):
        for copy in weights[level]:
            copy.start()

    row_index = lax.broadcasted_iota(jnp.int32, (lead, rows), 0)

    def prepare(level):
        for copy in weights[level]:
            copy.wait()
        for block in range(blocks):
            own_real = weight[level, 0, block]
            own_imag = weight[level, 1, block]
            own_matrix[level, block, :rows, :rows] = own_real
            own_matrix[level, block, :rows, rows:] = -own_imag
            own_matrix[level, block, rows:, :rows] = own_imag
            own_matrix[level, block, rows:, rows:] = own_real
            rank = jnp.where(coupling_ref[level, block] == 1, ranks_ref[level, block], 0)
            coupled = (row_index < rank).astype(jnp.float32)
            real = cross[level, 0, block].astype(jnp.float32) * coupled
            imag = cross[level, 1, block].astype(jnp.float32) * coupled
            cross_matrix[level, block, :rows] = jnp.concatenate([real, -imag], axis=0).T.astype(
                jnp.bfloat16
            )
            cross_matrix[level, block, rows:] = jnp.concatenate([imag, real], axis=0).T.astype(
                jnp.bfloat16
            )

    def apply(level, block, own, sibling):
        own = own.reshape(2 * rows, width)
        sibling = sibling.reshape(2 * lead, width)
        total = jnp.dot(own_matrix[level, block], own, preferred_element_type=jnp.float32)
        total += jnp.dot(cross_matrix[level, block], sibling, preferred_element_type=jnp.float32)
        return total.astype(jnp.bfloat16).reshape(2, rows, width)

    def send(step, chunk, block):
        return pltpu.make_async_remote_copy(
            src_ref=field.at[local + step, chunk, block, :, pl.ds(0, lead), :],
            dst_ref=arrived.at[step, chunk, block],
            send_sem=send_sem.at[step, chunk, block],
            recv_sem=recv_sem.at[step, chunk, block],
            device_id=partners[step],
            device_id_type=MESH,
        )

    def store_out(chunk, block):
        return pltpu.make_async_copy(
            result.at[chunk, block],
            out_ref.at[:, pl.ds(block * rows, rows), pl.ds(chunk * width, width)],
            out_sem.at[chunk, block],
        )

    selectors = []
    square = lax.broadcasted_iota(jnp.int32, (rows, rows), 0)
    for block in range(blocks):
        picked = square == order_ref[pl.ds(block, 1), :]
        selectors.append(picked.astype(jnp.float32).T.astype(jnp.bfloat16))

    for chunk in range(chunks):
        for block in range(blocks):
            panels[chunk][block].wait()
            for part in range(2):
                field[0, chunk, block, part] = jnp.dot(
                    selectors[block], panel[chunk, block, part], preferred_element_type=jnp.float32
                ).astype(jnp.bfloat16)
        for level in range(local):
            if chunk == 0:
                prepare(level)
            for block in range(blocks):
                field[level + 1, chunk, block] = apply(
                    level,
                    block,
                    field[level, chunk, block],
                    field[level, chunk, block ^ 2**level, :, :lead],
                )
                if level == local - 1:
                    if chunk == 0 and block == 0:
                        pl.semaphore_wait(barrier, len(partners))
                    send(0, chunk, block).start()
    for level in range(local, n_levels):
        prepare(level)

    def advance(step, unit):
        chunk, block = unit // blocks, unit % blocks
        level = local + step
        send(step, chunk, block).wait_recv()
        new = apply(level, block, field[level, chunk, block], arrived[step, chunk, block])
        if step < len(remote) - 1:
            field[level + 1, chunk, block] = new
            send(step + 1, chunk, block).start()
        else:
            result[chunk, block] = new
            store_out(chunk, block).start()

    units = chunks * blocks
    for turn in range(units + LAG * (len(remote) - 1)):
        for step in range(len(remote)):
            unit = turn - LAG * step
            if 0 <= unit < units:
                advance(step, unit)
    for chunk in range(chunks):
        for block in range(blocks):
            for step in range(len(remote)):
                send(step, chunk, block).wait_send()
            store_out(chunk, block).wait()


def shards(incident, self_weight, cross_weight, coupling, block_ranks, leaf_order):
    n_levels, _, blocks, rows, _ = self_weight.shape
    lead = cross_weight.shape[3]
    columns = incident.shape[2]
    width = min(WIDTH, columns)
    chunks = columns // width
    remote = remote_levels()
    far = len(remote)
    smem = pl.BlockSpec(memory_space=pltpu.SMEM)
    vmem = pl.BlockSpec(memory_space=pltpu.VMEM)
    anywhere = pl.BlockSpec(memory_space=pl.ANY)
    bf16 = jnp.bfloat16
    return pl.pallas_call(
        functools.partial(kernel, remote),
        out_shape=jax.ShapeDtypeStruct(incident.shape, bf16),
        in_specs=[smem, smem, vmem, anywhere, anywhere, anywhere],
        out_specs=anywhere,
        scratch_shapes=[
            pltpu.VMEM((chunks, blocks, 2, rows, width), bf16),
            pltpu.VMEM((n_levels, 2, blocks, rows, rows), bf16),
            pltpu.VMEM((n_levels, 2, blocks, lead, rows), bf16),
            pltpu.VMEM((n_levels, blocks, 2 * rows, 2 * rows), bf16),
            pltpu.VMEM((n_levels, blocks, 2 * rows, 2 * lead), bf16),
            pltpu.VMEM((n_levels, chunks, blocks, 2, rows, width), bf16),
            pltpu.VMEM((far, chunks, blocks, 2, lead, width), bf16),
            pltpu.VMEM((chunks, blocks, 2, rows, width), bf16),
            pltpu.SemaphoreType.DMA((chunks, blocks)),
            pltpu.SemaphoreType.DMA((n_levels,)),
            pltpu.SemaphoreType.DMA((n_levels,)),
            pltpu.SemaphoreType.DMA((far, chunks, blocks)),
            pltpu.SemaphoreType.DMA((far, chunks, blocks)),
            pltpu.SemaphoreType.DMA((chunks, blocks)),
        ],
        compiler_params=pltpu.CompilerParams(
            collective_id=0, has_side_effects=True, vmem_limit_bytes=48 * 2**20
        ),
    )(block_ranks, coupling, leaf_order, incident, self_weight, cross_weight)


def solution(mesh):
    in_specs = (
        P(None, ("leaf", "sub"), ("groups", "col")),
        P("groups", None, ("leaf", "sub"), None, None),
        P("groups", None, ("leaf", "sub"), None, None),
        P("groups", ("leaf", "sub")),
        P("groups", ("leaf", "sub")),
        P(("groups", "leaf", "sub"), None),
    )
    out_specs = P(None, ("leaf", "sub"), ("groups", "col"))
    return jax.shard_map(shards, mesh=mesh, in_specs=in_specs, out_specs=out_specs, check_vma=False)
```

```python
import functools

import jax
import jax.numpy as jnp
from jax import lax
from jax.experimental import pallas as pl
from jax.experimental.pallas import tpu as pltpu
from jax.sharding import PartitionSpec as P

MESH = pl.DeviceIdType.MESH
WIDTH = 256
LAG = 1
TAIL = 4
AHEAD = 3


def remote_levels():
    steps = []
    for axis in ("sub", "leaf"):
        for which_bit in range(lax.axis_size(axis).bit_length() - 1):
            steps.append((axis, 2**which_bit))
    return steps


def partner_of(axis, stride):
    me = lax.axis_index(axis)
    return {axis: me + stride * (1 - 2 * ((me // stride) % 2))}


def kernel(
    remote,
    ranks_ref,
    coupling_ref,
    order_ref,
    incident_ref,
    self_ref,
    cross_ref,
    out_ref,
    panel,
    weight,
    cross,
    own_matrix,
    cross_matrix,
    field,
    arrived,
    panel_sem,
    weight_sem,
    cross_sem,
    send_sem,
    recv_sem,
):
    n_levels, _, blocks, rows, _ = weight.shape
    lead = cross.shape[3]
    chunks = panel.shape[0]
    width = panel.shape[4]
    local = n_levels - len(remote)
    partners = [partner_of(axis, stride) for axis, stride in remote]

    barrier = pltpu.get_barrier_semaphore()
    for partner in partners:
        pl.semaphore_signal(barrier, inc=1, device_id=partner, device_id_type=MESH)

    def load_panel(chunk):
        columns = pl.ds(chunk * width, width)
        return [
            pltpu.make_async_copy(
                incident_ref.at[:, pl.ds(block * rows, rows), columns],
                panel.at[chunk, block],
                panel_sem.at[chunk, block],
            )
            for block in range(blocks)
        ]

    def load_weight(level):
        return [
            pltpu.make_async_copy(self_ref.at[level], weight.at[level], weight_sem.at[level]),
            pltpu.make_async_copy(cross_ref.at[level], cross.at[level], cross_sem.at[level]),
        ]

    panels = [load_panel(chunk) for chunk in range(chunks)]
    weights = [load_weight(level) for level in range(n_levels)]
    for copy in panels[0]:
        copy.start()
    for level in range(local):
        for copy in weights[level]:
            copy.start()
    for chunk in range(1, chunks):
        for copy in panels[chunk]:
            copy.start()
    for level in range(local, n_levels):
        for copy in weights[level]:
            copy.start()

    row_index = lax.broadcasted_iota(jnp.int32, (2 * lead, rows), 0)
    imag_half = lax.broadcasted_iota(jnp.int32, (rows, 2 * lead), 1) >= lead
    sign = jnp.where(imag_half, -1.0, 1.0).astype(jnp.bfloat16)

    def prepare(level):
        for copy in weights[level]:
            copy.wait()
        for block in range(blocks):
            own_real = weight[level, 0, block]
            own_imag = weight[level, 1, block]
            own_matrix[level, block, :rows, :rows] = own_real
            own_matrix[level, block, :rows, rows:] = -own_imag
            own_matrix[level, block, rows:, :rows] = own_imag
            own_matrix[level, block, rows:, rows:] = own_real
            at = (pl.ds(block, 1), pl.ds(level, 1))
            rank = jnp.where(coupling_ref[at] == 1, ranks_ref[at], 0)
            coupled = (row_index % lead < rank).astype(jnp.float32).astype(jnp.bfloat16)
            both = jnp.concatenate([cross[level, 0, block], cross[level, 1, block]], axis=0)
            both = (both * coupled).T
            cross_matrix[level, block, :rows] = both * sign
            cross_matrix[level, block, rows:] = jnp.concatenate([both[:, lead:], both[:, :lead]], axis=1)

    def apply(level, block, own, sibling):
        own = own.reshape(2 * rows, width)
        sibling = sibling.reshape(2 * lead, width)
        total = jnp.dot(own_matrix[level, block], own, preferred_element_type=jnp.float32)
        total += jnp.dot(cross_matrix[level, block], sibling, preferred_element_type=jnp.float32)
        return total.astype(jnp.bfloat16).reshape(2, rows, width)

    def send(step, chunk, block):
        return pltpu.make_async_remote_copy(
            src_ref=field.at[local + step, chunk, block, :, pl.ds(0, lead), :],
            dst_ref=arrived.at[step, chunk, block],
            send_sem=send_sem.at[step, chunk, block],
            recv_sem=recv_sem.at[step, chunk, block],
            device_id=partners[step],
            device_id_type=MESH,
        )

    selectors = []
    square = lax.broadcasted_iota(jnp.int32, (rows, rows), 0)
    for block in range(blocks):
        picked = square == order_ref[pl.ds(block, 1), :]
        selectors.append(picked.astype(jnp.float32).T.astype(jnp.bfloat16))

    for chunk in range(chunks):
        for block in range(blocks):
            panels[chunk][block].wait()
            for part in range(2):
                field[0, chunk, block, part] = jnp.dot(
                    selectors[block], panel[chunk, block, part], preferred_element_type=jnp.float32
                ).astype(jnp.bfloat16)
        for level in range(local):
            if chunk == 0:
                prepare(level)
            for block in range(blocks):
                field[level + 1, chunk, block] = apply(
                    level,
                    block,
                    field[level, chunk, block],
                    field[level, chunk, block ^ 2**level, :, :lead],
                )
                if level == local - 1:
                    if chunk == 0 and block == 0:
                        pl.semaphore_wait(barrier, len(partners))
                    if chunk * blocks + block < AHEAD:
                        send(0, chunk, block).start()
    def advance(step, unit):
        chunk, block = unit // blocks, unit % blocks
        level = local + step
        if unit == 0:
            prepare(level)
        send(step, chunk, block).wait_recv()
        new = apply(level, block, field[level, chunk, block], arrived[step, chunk, block])
        if step < len(remote) - 1:
            field[level + 1, chunk, block] = new
            send(step + 1, chunk, block).start()
        else:
            columns = pl.ds(chunk * width, width)
            out_ref[:, pl.ds(block * rows, rows), columns] = new

    units = chunks * blocks
    last = len(remote) - 1
    lags = [LAG * step + (TAIL if step == last else 0) for step in range(len(remote))]
    for turn in range(units + lags[last]):
        for step in range(len(remote)):
            unit = turn - lags[step]
            if 0 <= unit < units:
                advance(step, unit)
        if turn + AHEAD < units:
            send(0, (turn + AHEAD) // blocks, (turn + AHEAD) % blocks).start()
    for chunk in range(chunks):
        for block in range(blocks):
            for step in range(len(remote)):
                send(step, chunk, block).wait_send()


def shards(incident, self_weight, cross_weight, coupling, block_ranks, leaf_order):
    n_levels, _, blocks, rows, _ = self_weight.shape
    lead = cross_weight.shape[3]
    columns = incident.shape[2]
    width = min(WIDTH, columns)
    chunks = columns // width
    remote = remote_levels()
    far = len(remote)
    vmem = pl.BlockSpec(memory_space=pltpu.VMEM)
    hbm = pl.BlockSpec(memory_space=pltpu.HBM)
    bf16 = jnp.bfloat16
    return pl.pallas_call(
        functools.partial(kernel, remote),
        out_shape=pltpu.VMEM(incident.shape, bf16),
        in_specs=[vmem, vmem, vmem, hbm, hbm, hbm],
        out_specs=vmem,
        scratch_shapes=[
            pltpu.VMEM((chunks, blocks, 2, rows, width), bf16),
            pltpu.VMEM((n_levels, 2, blocks, rows, rows), bf16),
            pltpu.VMEM((n_levels, 2, blocks, lead, rows), bf16),
            pltpu.VMEM((n_levels, blocks, 2 * rows, 2 * rows), bf16),
            pltpu.VMEM((n_levels, blocks, 2 * rows, 2 * lead), bf16),
            pltpu.VMEM((n_levels, chunks, blocks, 2, rows, width), bf16),
            pltpu.VMEM((far, chunks, blocks, 2, lead, width), bf16),
            pltpu.SemaphoreType.DMA((chunks, blocks)),
            pltpu.SemaphoreType.DMA((n_levels,)),
            pltpu.SemaphoreType.DMA((n_levels,)),
            pltpu.SemaphoreType.DMA((far, chunks, blocks)),
            pltpu.SemaphoreType.DMA((far, chunks, blocks)),
        ],
        compiler_params=pltpu.CompilerParams(
            collective_id=0, has_side_effects=True, vmem_limit_bytes=60 * 2**20
        ),
    )(block_ranks.T, coupling.T, leaf_order, incident, self_weight, cross_weight)


def solution(mesh):
    in_specs = (
        P(None, ("leaf", "sub"), ("groups", "col")),
        P("groups", None, ("leaf", "sub"), None, None),
        P("groups", None, ("leaf", "sub"), None, None),
        P("groups", ("leaf", "sub")),
        P("groups", ("leaf", "sub")),
        P(("groups", "leaf", "sub"), None),
    )
    out_specs = P(None, ("leaf", "sub"), ("groups", "col"))
    return jax.shard_map(shards, mesh=mesh, in_specs=in_specs, out_specs=out_specs, check_vma=False)
```
